32 devices in a mesh: vert: 16 (over z, x, core), row: 2 (over y).
Axes of the slice: x: 2, y: 2, z: 4, core: 2. Of those that a mesh axis runs over, the one named last changes fastest.
Arguments:
- features: float32 [131072, 256], P(('vert', 'row')), may hold values from -6 to 6
- w_self: float32 [256, 256], replicated, may hold values from -0.375 to 0.375
- w_neigh: float32 [256, 256], replicated, may hold values from -0.75 to 0.75
- bias: float32 [256], replicated, may hold values from -3 to 3
- w_head: float32 [256], replicated, may hold values from -0.75 to 0.75
- tile_weights: float32 [4096, 128, 128], P(('vert', 'row')), may hold values from 0.01 to 1
- tile_dst: int32 [4096], P(('vert', 'row')), may hold values from 0 to 31
- tile_src: int32 [4096], P(('vert', 'row')), may hold values from 0 to 65
- tile_count: int32 [32], P(('vert', 'row')), may hold values from 16 to 128, as said below
- hub_block: int32 [32], P(('vert', 'row')), may hold values from 0 to 31
- send_rows: int32 [32, 32, 8], P(('vert', 'row')), may hold values from 0 to 4095
- send_count: int32 [32, 32], P(('vert', 'row')), may hold values from 1 to 8, as said below
- labels: int32 [131072], P(('vert', 'row')), may hold values from 0 to 1
Outputs:
- grad_self: float32 [256, 256], replicated
- grad_neigh: float32 [256, 256], replicated
- grad_bias: float32 [256], replicated
- grad_head: float32 [256], replicated
The draws below stay inside these ranges and needn't reach their ends.
Inputs may be any that keep to these rules, and one draw needn't show every extreme that they name: Tile t of a device is used when t < its tile_count; some device uses all 128 tiles and some 128 // 8. `send_count`: each sending device fills all 8 slots for at least one receiving device.
All inputs are finite; a program needn't handle non-finite values.
Results may differ from the reference program's by a relative error of at most 0.0003.
Values sent between devices are 32-bit elements; how exact they have to be, the bound alone decides.
No kernel may reach another device: no remote copies, remote signals or barrier semaphores. Data moves between devices by JAX's collectives and lax.ppermute only.
A program may use at most 128 MiB of HBM per device.

```python
import math
import jax
import jax.numpy as jnp
from jax import lax

F = 256
BLK = 128
NB = 32
TILES = 128
CAP = 8
PEERS = 32
VERTS = 131072
SRC = 66


def draw_tile_count(key, part):
    first_key, second_key = jax.random.split(key)
    shifts = jax.random.randint(first_key, (PEERS,), 0, 4)
    counts = TILES // jnp.left_shift(jnp.ones((PEERS,), jnp.int32), shifts)
    order = jax.random.permutation(second_key, PEERS)
    counts = counts.at[order[0]].set(TILES)
    counts = counts.at[order[1]].set(TILES // 8)
    return counts.astype(jnp.int32)


def draw_send_count(key, part):
    first_key, second_key = jax.random.split(key)
    counts = jax.random.randint(first_key, (PEERS, PEERS), 1, CAP + 1)
    full_peer = jax.random.randint(second_key, (PEERS,), 0, PEERS)
    columns = jnp.arange(PEERS, dtype=jnp.int32)
    counts = jnp.where(columns[None, :] == full_peer[:, None], CAP, counts)
    return counts.astype(jnp.int32)


def touch_ends(array, own_key, smallest, top_value):
    longest = array.shape.index(max(array.shape))
    spots = []
    for shift in (0, 1):
        where = [jax.random.randint(jax.random.fold_in(own_key, axis), (), 0, length) for axis, length in enumerate(array.shape)]
        where[longest] = (where[longest] + shift) % array.shape[longest]
        spots.append(tuple(where))
    return array.at[spots[0]].set(smallest).at[spots[1]].set(top_value)


def block_scale(own_key, extent, cuts, smallest, top_value):
    level, own = 1.0, jax.random.fold_in(own_key, 6)
    for dim, parts in cuts:
        steps = jnp.exp(jax.random.uniform(jax.random.fold_in(own, dim), (parts,), jnp.float32, smallest / len(cuts), top_value / len(cuts)))
        level = level * jnp.repeat(steps, extent[dim] // parts).reshape([-1 if axis == dim else 1 for axis in range(len(extent))])
    return level


def scatter_about(own_key, shape, spread, limit, shards=(), held_as=jnp.bfloat16):
    entries = spread * jax.random.normal(own_key, shape, jnp.float32)
    if shards:
        entries = entries * block_scale(own_key, shape, shards, -0.22, 0.18)
    return jnp.clip(entries, -limit, limit).astype(held_as)


def setup_inputs(seed: int = 0) -> dict:
    seeds = jax.random.split(jax.random.key(seed), 14)
    return {
        "features": scatter_about(seeds[0], (VERTS, F), 1.0, 6.0, ((0, 32),), jnp.float32),
        "w_self": scatter_about(seeds[1], (F, F), F ** -0.5, 0.375, (), jnp.float32),
        "w_neigh": scatter_about(seeds[2], (F, F), (F // 4) ** -0.5, 0.75, (), jnp.float32),
        "bias": scatter_about(seeds[3], (F,), 0.5, 3.0, (), jnp.float32),
        "w_head": scatter_about(seeds[4], (F,), (F // 4) ** -0.5, 0.75, (), jnp.float32),
        "tile_weights": jnp.clip(jnp.exp(math.log(1.0) - 4.6051702 * jax.random.uniform(seeds[5], (PEERS * TILES, BLK, BLK), jnp.float32) ** block_scale(seeds[5], (PEERS * TILES, BLK, BLK), ((0, 32),), -0.2, 0.2)), 0.01, 1.0),
        "tile_dst": touch_ends(jax.random.randint(seeds[6], (PEERS * TILES,), 0, NB), jax.random.fold_in(seeds[6], 1), 0, NB - 1).astype(jnp.int32),
        "tile_src": touch_ends(jax.random.randint(seeds[7], (PEERS * TILES,), 0, SRC), jax.random.fold_in(seeds[7], 1), 0, SRC - 1).astype(jnp.int32),
        "tile_count": draw_tile_count(jax.random.fold_in(seeds[13], 71), 0),
        "hub_block": touch_ends(jax.random.randint(seeds[9], (PEERS,), 0, NB), jax.random.fold_in(seeds[9], 1), 0, NB - 1).astype(jnp.int32),
        "send_rows": touch_ends(jax.random.randint(seeds[10], (PEERS, PEERS, CAP), 0, NB * BLK), jax.random.fold_in(seeds[10], 1), 0, (NB * BLK) - 1).astype(jnp.int32),
        "send_count": draw_send_count(jax.random.fold_in(seeds[13], 71), 0),
        "labels": touch_ends(jax.random.randint(seeds[12], (VERTS,), 0, 2), jax.random.fold_in(seeds[12], 1), 0, 1).astype(jnp.int32),
    }


FULL_PRECISION = lax.Precision.HIGHEST

def reference(features, w_self, w_neigh, bias, w_head, tile_weights, tile_dst, tile_src, tile_count, hub_block, send_rows, send_count, labels):
    feats_three = features.reshape(PEERS, NB * BLK, F)
    blocks_four = features.reshape(PEERS, NB, BLK, F)
    device_ids = jnp.arange(PEERS, dtype=jnp.int32)
    hub_blocks = blocks_four[device_ids, hub_block]
    slot_index = jnp.arange(CAP, dtype=jnp.int32)
    block_ids = jnp.arange(NB, dtype=jnp.int32)
    tile_ids = jnp.arange(TILES, dtype=jnp.int32)

    def per_device(device):
        own_blocks = lax.dynamic_index_in_dim(blocks_four, device, 0, keepdims=False)
        listed = lax.dynamic_index_in_dim(send_rows, device, 1, keepdims=False)
        counts = lax.dynamic_index_in_dim(send_count, device, 1, keepdims=False)
        border = feats_three[device_ids[:, None], listed]
        alive = slot_index[None, :] < counts[:, None]
        border = jnp.where(alive[:, :, None], border, jnp.zeros_like(border))
        source_table = jnp.concatenate([own_blocks, border.reshape(-1, BLK, F), hub_blocks], 0)
        start = (device * TILES).astype(jnp.int32)
        weights_here = lax.dynamic_slice_in_dim(tile_weights, start, TILES, 0)
        dst_here = lax.dynamic_slice_in_dim(tile_dst, start, TILES, 0)
        src_here = lax.dynamic_slice_in_dim(tile_src, start, TILES, 0)
        count_here = lax.dynamic_index_in_dim(tile_count, device, 0, keepdims=False)
        active = tile_ids < count_here
        picked = source_table[src_here]
        contrib = jnp.einsum('tij,tjf->tif', weights_here, picked, precision=FULL_PRECISION)
        selector = ((dst_here[None, :] == block_ids[:, None]) & active[None, :]).astype(features.dtype)
        summed = jnp.einsum('bt,tif->bif', selector, contrib, precision=FULL_PRECISION)
        weight_sum = jnp.einsum('bt,ti->bi', selector, lax.optimization_barrier(jnp.sum(weights_here, axis=2)), precision=FULL_PRECISION)
        neigh_mean = (own_blocks + summed) / (1.0 + weight_sum)[:, :, None]
        return neigh_mean.reshape(NB * BLK, F)
    neigh_mean = lax.map(per_device, device_ids).reshape(VERTS, F)
    pre_act = jnp.dot(features, w_self, precision=FULL_PRECISION) + jnp.dot(neigh_mean, w_neigh, precision=FULL_PRECISION) + bias[None, :]
    sigmoid_pre = jax.nn.sigmoid(pre_act)
    hidden = pre_act * sigmoid_pre
    head_score = jnp.dot(hidden, w_head, precision=FULL_PRECISION)
    target = 2.0 * labels.astype(features.dtype) - 1.0
    loss_scale = 1.0 / math.sqrt(VERTS)
    dscore = (head_score - target) * loss_scale
    dpre = dscore[:, None] * w_head[None, :] * (sigmoid_pre * (1.0 + pre_act * (1.0 - sigmoid_pre)))
    grad_self = jnp.dot(features.T, dpre, precision=FULL_PRECISION)
    grad_neigh = jnp.dot(neigh_mean.T, dpre, precision=FULL_PRECISION)
    grad_bias = lax.optimization_barrier(jnp.sum(dpre, axis=0))
    grad_head = jnp.dot(hidden.T, dscore, precision=FULL_PRECISION)
    return (grad_self, grad_neigh, grad_bias, grad_head)
```

```python
import functools
import math

import jax
import jax.numpy as jnp
from jax import lax
from jax.experimental import pallas as pl
from jax.experimental.pallas import tpu as pltpu
from jax.sharding import PartitionSpec as P

AXES = ("vert", "row")
F32 = jnp.float32
BF16 = jnp.bfloat16
BUFFERS = 16
GROUP = 4
CHUNK = 512
VMEM_BYTES = 40 * 1024 * 1024


def split(x):
    hi = x.astype(BF16)
    return hi, (x - hi.astype(F32)).astype(BF16)


def dot(a, b, contract=((1,), (0,))):
    return lax.dot_general(a, b, (contract, ((), ())), preferred_element_type=F32)


def dot3(a, b, contract=((1,), (0,))):
    (a_hi, a_lo), (b_hi, b_lo) = a, b
    return dot(a_hi, b_hi, contract) + dot(a_hi, b_lo, contract) + dot(a_lo, b_hi, contract)


def tile_product(weights, source):
    w_hi, w_lo = split(weights)
    s_hi, s_lo = split(source)
    wide = jnp.concatenate([w_hi, w_hi], 1)
    tall = jnp.concatenate([s_hi, s_lo], 0)
    return dot(wide, tall) + dot(w_lo, s_hi)


def stream_tiles(total, tile_of, weights_ref, buffer_ref, sems, use):
    depth = buffer_ref.shape[0] // GROUP

    def copies(group):
        base = lax.rem(group, depth) * GROUP
        for k in range(GROUP):
            i = jnp.minimum(group * GROUP + k, total - 1)
            yield pltpu.make_async_copy(weights_ref.at[tile_of(i)], buffer_ref.at[base + k], sems.at[base + k])

    groups = (total + GROUP - 1) // GROUP

    for ahead in range(depth):
        @pl.when(ahead < groups)
        def _():
            for copy in copies(jnp.int32(ahead)):
                copy.start()

    def step(group, carry):
        for copy in copies(group):
            copy.wait()
        base = lax.rem(group, depth) * GROUP
        at = [jnp.minimum(group * GROUP + k, total - 1) for k in range(GROUP)]
        use(at, [buffer_ref[base + k] for k in range(GROUP)], [group * GROUP + k < total for k in range(GROUP)])

        @pl.when(group + depth < groups)
        def _():
            for copy in copies(group + depth):
                copy.start()

        return carry

    lax.fori_loop(0, groups, step, 0)


def add_tiles(list_ref, weights_ref, buffer_ref, sems, source_of, acc_ref):
    size = buffer_ref.shape[1]
    total = list_ref[list_ref.shape[0] - 7]

    def use(at, weights, live):
        entries = [list_ref[i] for i in at]
        products = [tile_product(w, source_of(entry // 16384)) for w, entry in zip(weights, entries)]
        for entry, product, alive in zip(entries, products, live):
            block = lax.rem(entry // 256, 64)
            where = pl.ds(pl.multiple_of(block * size, size), size)

            @pl.when(alive)
            def _():
                acc_ref[where, :] += product

    stream_tiles(total, lambda i: lax.rem(list_ref[i], 256), weights_ref, buffer_ref, sems, use)


def own_kernel(
    dst_ref, code_ref, count_ref, rows_ref, used_ref, features_ref, weights_ref,
    acc_ref, outgoing_ref, early_ref, late_ref,
    own_ref, buffer_ref, sems,
):
    tiles = dst_ref.shape[0]
    size = buffer_ref.shape[1]
    peers = used_ref.shape[0]
    slots = rows_ref.shape[0] // peers
    lists = (own_ref, early_ref, late_ref)

    def sort(t, counts):
        code = code_ref[t]
        stage = code // 65536
        entry = (lax.rem(code, 65536) * 64 + dst_ref[t]) * 256 + t
        for ref, count in zip(lists, counts):
            ref[count] = entry
        return tuple(count + jnp.where(stage == i, 1, 0) for i, count in enumerate(counts))

    counts = lax.fori_loop(0, count_ref[0], sort, (jnp.int32(0),) * 3)
    for ref, count in zip(lists, counts):
        ref[tiles + 1] = count

    acc_ref[...] = features_ref[...]

    def gather(peer, carry):
        for k in range(slots):
            row = features_ref[pl.ds(rows_ref[peer * slots + k], 1), :]
            outgoing_ref[peer, k : k + 1, :] = jnp.where(k < used_ref[peer], row, 0.0)
        return carry

    lax.fori_loop(0, peers, gather, 0)

    def source_of(block):
        return features_ref[pl.ds(pl.multiple_of(block * size, size), size), :]

    add_tiles(own_ref, weights_ref, buffer_ref, sems, source_of, acc_ref)


def own_dense_kernel(
    dst_ref, count_ref, features_ref, weights_ref, w_self_ref, bias_ref, labels_ref,
    pre_ref, aux_ref,
    buffer_ref, weight_acc_ref, sems,
):
    blocks, size, _ = weight_acc_ref.shape
    weight_acc_ref[...] = jnp.zeros_like(weight_acc_ref)

    def use(at, weights, live):
        for i, w, alive in zip(at, weights, live):
            @pl.when(alive)
            def _():
                weight_acc_ref[dst_ref[i]] += w

    stream_tiles(count_ref[0], lambda i: i, weights_ref, buffer_ref, sems, use)

    eye = lax.broadcasted_iota(jnp.int32, (size, size), 0) == lax.broadcasted_iota(jnp.int32, (size, size), 1)
    left = lax.broadcasted_iota(jnp.int32, (size, size), 1) < size // 2

    def columns(block, carry):
        inverse = 1.0 / (1.0 + jnp.sum(weight_acc_ref[block], axis=1, keepdims=True))
        target = 2.0 * labels_ref[pl.ds(block, 1), :].astype(F32) - 1.0
        target = jnp.sum(jnp.where(eye, jnp.broadcast_to(target, eye.shape), 0.0), axis=1, keepdims=True)
        aux_ref[pl.ds(pl.multiple_of(block * size, size), size), :] = jnp.where(left, inverse, target)
        return carry

    lax.fori_loop(0, blocks, columns, 0)

    w_self = split(w_self_ref[...])

    def dense(i, carry):
        where = pl.ds(pl.multiple_of(i * CHUNK, CHUNK), CHUNK)
        pre_ref[where, :] = dot3(split(features_ref[where, :]), w_self) + bias_ref[...]
        return carry

    lax.fori_loop(0, features_ref.shape[0] // CHUNK, dense, 0)


def early_kernel(
    list_ref, border_ref, mine_ref, far_ref, other_ref, far_other_ref, acc_in_ref, weights_ref, acc_ref,
    buffer_ref, sources_ref, sems, load_sems,
):
    del acc_in_ref
    at, copies = 0, []
    for i, part in enumerate((border_ref, mine_ref, far_ref, other_ref, far_other_ref)):
        blocks = part.shape[0]
        copies.append(pltpu.make_async_copy(part, sources_ref.at[pl.ds(at, blocks)], load_sems.at[i]))
        at += blocks
    for copy in copies:
        copy.start()
    for copy in copies:
        copy.wait()
    add_tiles(list_ref, weights_ref, buffer_ref, sems, lambda i: sources_ref[i], acc_ref)


def late_kernel(
    list_ref, place_ref, mine_ref, other_ref, acc_in_ref, weights_ref,
    features_ref, pre_ref, aux_ref, w_neigh_ref, w_head_ref,
    keep_ref, send_ref,
    buffer_ref, sources_ref, acc_ref, feat_ref, base_ref, col_ref, total_ref, bias_ref, head_ref,
    sems, load_sems, *, scale,
):
    blocks = mine_ref.shape[0]
    loads = [
        (mine_ref, sources_ref.at[pl.ds(0, blocks)]),
        (other_ref, sources_ref.at[pl.ds(blocks, blocks)]),
        (acc_in_ref, acc_ref),
        (features_ref, feat_ref),
        (pre_ref, base_ref),
        (aux_ref, col_ref),
    ]
    copies = [pltpu.make_async_copy(a, b, load_sems.at[i]) for i, (a, b) in enumerate(loads)]
    for copy in copies:
        copy.start()
    total_ref[...] = jnp.zeros_like(total_ref)
    bias_ref[...] = jnp.zeros_like(bias_ref)
    head_ref[...] = jnp.zeros_like(head_ref)
    w_neigh = split(w_neigh_ref[...])
    w_head = w_head_ref[...]
    for copy in copies[:3]:
        copy.wait()
    add_tiles(list_ref, weights_ref, buffer_ref, sems, lambda i: sources_ref[i], acc_ref)
    for copy in copies[3:]:
        copy.wait()
    width = feat_ref.shape[1]
    half = col_ref.shape[1] // 2

    def dense(i, carry):
        where = pl.ds(pl.multiple_of(i * CHUNK, CHUNK), CHUNK)
        columns = col_ref[where, :]
        mean = split(acc_ref[where, :] * columns[:, 0:1])
        pre = base_ref[where, :] + dot3(mean, w_neigh)
        sig = jax.nn.sigmoid(pre)
        hidden = pre * sig
        score = jnp.sum(hidden * w_head, axis=1, keepdims=True)
        dscore = (score - columns[:, half : half + 1]) * scale
        dpre = dscore * w_head * (sig * (1.0 + pre * (1.0 - sig)))
        bias_ref[...] += jnp.sum(dpre.reshape(CHUNK // 8, 8, width), axis=0)
        head_ref[...] += jnp.sum((hidden * dscore).reshape(CHUNK // 8, 8, width), axis=0)
        dpre = split(dpre)
        total_ref[0:width, :] += dot3(split(feat_ref[where, :]), dpre, ((0,), (0,)))
        total_ref[width : 2 * width, :] += dot3(mean, dpre, ((0,), (0,)))
        return carry

    lax.fori_loop(0, feat_ref.shape[0] // CHUNK, dense, 0)

    me = place_ref[0]
    rows = 2 * width // 8
    extra = keep_ref.shape[1] - rows
    row_ids = lax.broadcasted_iota(jnp.int32, (extra, width), 0)
    vectors = jnp.where(row_ids == 0, jnp.sum(bias_ref[...], axis=0, keepdims=True), 0.0)
    vectors = jnp.where(row_ids == 1, jnp.sum(head_ref[...], axis=0, keepdims=True), vectors)
    for ref, away in ((keep_ref, 0), (send_ref, 4)):
        for j in range(4):
            piece = me ^ (away + j)
            ref[j, 0:rows, :] = total_ref[pl.ds(pl.multiple_of(piece * rows, rows), rows), :]
            ref[j, rows:, :] = jnp.where(piece == 0, vectors, 0.0)


def finish_kernel(place_ref, mine_ref, other_ref, self_ref, neigh_ref, bias_ref, head_ref):
    me = place_ref[0]
    width = self_ref.shape[1]
    rows = 2 * width // 8
    for ref, away in ((mine_ref, 0), (other_ref, 4)):
        for j in range(4):
            piece = me ^ (away + j)
            part = ref[j, 0:rows, :]
            at = pl.ds(pl.multiple_of(lax.rem(piece, 4) * rows, rows), rows)

            @pl.when(piece < 4)
            def _():
                self_ref[at, :] = part

            @pl.when(piece >= 4)
            def _():
                neigh_ref[at, :] = part

            @pl.when(piece == 0)
            def _():
                bias_ref[...] = ref[j, rows : rows + 1, :]
                head_ref[...] = ref[j, rows + 1 : rows + 2, :]


def shape(*dims, dtype=F32):
    return jax.ShapeDtypeStruct(dims, dtype)


SMEM = pl.BlockSpec(memory_space=pltpu.SMEM)
VMEM = pl.BlockSpec(memory_space=pltpu.VMEM)
ANY = pl.BlockSpec(memory_space=pl.ANY)


def on_device(
    peers,
    features,
    w_self,
    w_neigh,
    bias,
    w_head,
    tile_weights,
    tile_dst,
    tile_src,
    tile_count,
    hub_block,
    send_rows,
    send_count,
    labels,
):
    tiles, size, _ = tile_weights.shape
    verts, width = features.shape
    blocks = verts // size
    slots = send_rows.shape[2]
    border_blocks = peers * slots // size
    me = (lax.axis_index("vert") * lax.axis_size("row") + lax.axis_index("row")).astype(jnp.int32)

    bits = peers.bit_length() - 1
    core = 2
    line = [k << (bits - 2) for k in (1, 2, 3)]
    plane = [1 << b for b in range(bits - 2) if 1 << b != core]
    order = (plane[::-1], plane)

    def across(x, mask_of):
        return lax.ppermute(x, AXES, [(i, i ^ mask_of(i)) for i in range(peers)])

    source = tile_src.astype(jnp.int32)
    hub = jnp.clip(source - blocks - border_blocks, 0, peers - 1)
    apart = hub ^ me
    place_in_line = apart >> (bits - 2)
    sender_core = (hub >> 1) & 1
    steps = len(plane)

    def differs(s):
        return jnp.where(sender_core == 0, apart & order[0][s], apart & order[1][s]) != 0

    held_blocks, far_blocks = peers // 4, peers // 8
    index = place_in_line
    for s in range(steps - 1):
        index = index + jnp.where(differs(s), 4 << s, 0)
    through = differs(steps - 1)
    late = through & (index >= far_blocks)
    early_code = 65536 + border_blocks + index + jnp.where(through, held_blocks, 0)
    early_code = early_code + jnp.where((apart & core) != 0, held_blocks + far_blocks, 0)
    late_code = 2 * 65536 + index - far_blocks + jnp.where((apart & core) != 0, far_blocks, 0)
    code = jnp.where(late, late_code, early_code)
    code = jnp.where(source < blocks + border_blocks, 65536 + source - blocks, code)
    code = jnp.where(source < blocks, source, code)

    mine = lax.dynamic_slice_in_dim(features, hub_block[0] * size, size, 0)[None]
    held = jnp.concatenate([mine] + [across(mine, lambda i, m=m: m) for m in line], 0)

    acc, outgoing, early_list, late_list = pl.pallas_call(
        own_kernel,
        out_shape=(
            shape(verts, width),
            shape(peers, slots, width),
            shape(tiles + 8, dtype=jnp.int32),
            shape(tiles + 8, dtype=jnp.int32),
        ),
        in_specs=[SMEM] * 5 + [VMEM, ANY],
        out_specs=(VMEM, VMEM, SMEM, SMEM),
        scratch_shapes=[
            pltpu.SMEM((tiles + 8,), jnp.int32),
            pltpu.VMEM((BUFFERS, size, size), F32),
            pltpu.SemaphoreType.DMA((BUFFERS,)),
        ],
        compiler_params=pltpu.CompilerParams(vmem_limit_bytes=VMEM_BYTES),
        cost_estimate=pl.CostEstimate(flops=8_000_000_000, bytes_accessed=24_000_000, transcendentals=0),
        name="own_tiles",
    )(
        tile_dst, code, tile_count, send_rows.reshape(-1), send_count.reshape(-1),
        features, tile_weights,
    )
    held, acc, outgoing = lax.optimization_barrier((held, acc, outgoing))

    pre, aux = pl.pallas_call(
        own_dense_kernel,
        out_shape=(shape(verts, width), shape(verts, size)),
        in_specs=[SMEM] * 2 + [VMEM, ANY, VMEM, VMEM, VMEM],
        out_specs=(VMEM, VMEM),
        scratch_shapes=[
            pltpu.VMEM((BUFFERS, size, size), F32),
            pltpu.VMEM((blocks, size, size), F32),
            pltpu.SemaphoreType.DMA((BUFFERS,)),
        ],
        compiler_params=pltpu.CompilerParams(vmem_limit_bytes=VMEM_BYTES),
        cost_estimate=pl.CostEstimate(flops=6_000_000_000, bytes_accessed=18_000_000, transcendentals=0),
        name="own_dense",
    )(
        tile_dst, tile_count, features, tile_weights, w_self, bias.reshape(1, width),
        labels.reshape(blocks, size),
    )

    incoming = lax.all_to_all(outgoing, AXES, split_axis=0, concat_axis=0, tiled=True)
    border = incoming.reshape(border_blocks, size, width)

    for s in range(steps - 1):
        near = held
        held = jnp.concatenate([held, across(held, lambda i, s=s: order[(i >> 1) & 1][s])], 0)
    far_near = across(near, lambda i: order[(i >> 1) & 1][steps - 1])
    held, far_near, border, pre, aux = lax.optimization_barrier((held, far_near, border, pre, aux))
    far = across(held[far_blocks:], lambda i: order[(i >> 1) & 1][steps - 1])
    held_other = across(held, lambda i: core)
    far_near_other = across(far_near, lambda i: core)

    acc = pl.pallas_call(
        early_kernel,
        out_shape=shape(verts, width),
        in_specs=[SMEM] + [ANY] * 5 + [VMEM, ANY],
        out_specs=VMEM,
        scratch_shapes=[
            pltpu.VMEM((BUFFERS, size, size), F32),
            pltpu.VMEM((border_blocks + 2 * (held_blocks + far_blocks), size, width), F32),
            pltpu.SemaphoreType.DMA((BUFFERS,)),
            pltpu.SemaphoreType.DMA((5,)),
        ],
        input_output_aliases={6: 0},
        compiler_params=pltpu.CompilerParams(vmem_limit_bytes=VMEM_BYTES),
        cost_estimate=pl.CostEstimate(flops=6_000_000_000, bytes_accessed=12_000_000, transcendentals=0),
        name="early_tiles",
    )(early_list, border, held, far_near, held_other, far_near_other, acc, tile_weights)
    far, acc = lax.optimization_barrier((far, acc))
    far_other = across(far, lambda i: core)

    place = ((me >> 1) & 1) * 4 + ((me >> 2) & 1) * 2 + (me & 1)
    place = place.reshape(1)
    piece_rows = 2 * width // 8 + 8
    keep, send = pl.pallas_call(
        functools.partial(late_kernel, scale=1.0 / math.sqrt(verts * peers)),
        out_shape=(shape(4, piece_rows, width), shape(4, piece_rows, width)),
        in_specs=[SMEM, SMEM] + [ANY] * 7 + [VMEM, VMEM],
        out_specs=(VMEM, VMEM),
        scratch_shapes=[
            pltpu.VMEM((BUFFERS, size, size), F32),
            pltpu.VMEM((2 * far_blocks, size, width), F32),
            pltpu.VMEM((verts, width), F32),
            pltpu.VMEM((verts, width), F32),
            pltpu.VMEM((verts, width), F32),
            pltpu.VMEM((verts, size), F32),
            pltpu.VMEM((2 * width, width), F32),
            pltpu.VMEM((8, width), F32),
            pltpu.VMEM((8, width), F32),
            pltpu.SemaphoreType.DMA((BUFFERS,)),
            pltpu.SemaphoreType.DMA((6,)),
        ],
        compiler_params=pltpu.CompilerParams(vmem_limit_bytes=VMEM_BYTES),
        cost_estimate=pl.CostEstimate(flops=12_000_000_000, bytes_accessed=20_000_000, transcendentals=0),
        name="late_tiles_and_gradients",
    )(
        late_list, place, far, far_other, acc, tile_weights, features, pre, aux,
        w_neigh, w_head.reshape(1, width),
    )

    held = keep + across(send, lambda i: core)
    reach = (0, 1, 4, 5)
    got = [held[0]] + [across(held[j], lambda i, j=j: reach[j]) for j in (1, 2, 3)]
    total = (got[0] + got[1]) + (got[2] + got[3])
    for low in range(3, bits, 2):
        masks = [1 << low] if low + 1 == bits else [k << low for k in (1, 2, 3)]
        more = [across(total, lambda i, m=m: m) for m in masks]
        total = total + more[0] if len(more) == 1 else (total + more[0]) + (more[1] + more[2])
    mine = jnp.stack([total] + [across(total, lambda i, j=j: reach[j]) for j in (1, 2, 3)])
    other = across(mine, lambda i: core)
    grad_self, grad_neigh, grad_bias, grad_head = pl.pallas_call(
        finish_kernel,
        out_shape=(shape(width, width), shape(width, width), shape(1, width), shape(1, width)),
        in_specs=[SMEM, VMEM, VMEM],
        out_specs=(VMEM, VMEM, VMEM, VMEM),
        name="assemble",
    )(place, mine, other)
    return (grad_self, grad_neigh, grad_bias.reshape(width), grad_head.reshape(width))


def solution(mesh):
    peers = math.prod(mesh.shape.values())
    in_specs = (
        P(AXES, None),
        P(),
        P(),
        P(),
        P(),
        P(AXES, None, None),
        P(AXES),
        P(AXES),
        P(AXES),
        P(AXES),
        P(AXES, None, None),
        P(AXES, None),
        P(AXES),
    )
    out_specs = (P(), P(), P(), P())
    return jax.shard_map(
        functools.partial(on_device, peers),
        mesh=mesh,
        in_specs=in_specs,
        out_specs=out_specs,
        check_vma=False,
    )
```

```python
import functools
import math

import jax
import jax.numpy as jnp
from jax import lax
from jax.experimental import pallas as pl
from jax.experimental.pallas import tpu as pltpu
from jax.sharding import PartitionSpec as P

AXES = ("vert", "row")
F32 = jnp.float32
BF16 = jnp.bfloat16
LOADS = 8
GROUP = 8
CHUNK = 512
UNROLL = 4
COST = pl.CostEstimate(flops=1_000_000, bytes_accessed=100_000, transcendentals=0)
VMEM_BYTES = 44 * 1024 * 1024


def split(x):
    hi = x.astype(BF16)
    return hi, (x - hi.astype(F32)).astype(BF16)


def dot(a, b, contract=((1,), (0,))):
    return lax.dot_general(a, b, (contract, ((), ())), preferred_element_type=F32)


def dot3(a, b, contract=((1,), (0,))):
    (a_hi, a_lo), (b_hi, b_lo) = a, b
    return dot(a_hi, b_hi, contract) + dot(a_hi, b_lo, contract) + dot(a_lo, b_hi, contract)


def tile_product(weights, source):
    w_hi, w_lo = split(weights)
    s_hi, s_lo = split(source)
    wide = jnp.concatenate([w_hi, w_hi], 1)
    tall = jnp.concatenate([s_hi, s_lo], 0)
    return dot(wide, tall) + dot(w_lo, s_hi)


def add_tiles(list_ref, weights_ref, source_of, acc_ref, tile_of, ready):
    size = weights_ref.shape[1]
    total = list_ref[list_ref.shape[0] - 7]

    def step(group, carry):
        at = [group * GROUP + k for k in range(GROUP)]
        for i in at:
            ready(i, total)
        capped = [jnp.minimum(i, total - 1) for i in at]
        entries = [list_ref[i] for i in capped]
        products = [
            tile_product(weights_ref[tile_of(i, entry)], source_of(entry // 16384))
            for i, entry in zip(capped, entries)
        ]
        for i, entry, product in zip(at, entries, products):
            block = lax.rem(entry // 256, 64)
            where = pl.ds(pl.multiple_of(block * size, size), size)
            acc_ref[where, :] += jnp.where(i < total, product, 0.0)
        return carry

    lax.fori_loop(0, (total + GROUP - 1) // GROUP, step, 0)


def fetch_tiles(list_ref, weights_in_ref, weights_ref, sems):
    def copy(i):
        return pltpu.make_async_copy(
            weights_in_ref.at[lax.rem(list_ref[i], 256)], weights_ref.at[i], sems.at[i]
        )

    def start(i, carry):
        copy(i).start()
        return carry

    lax.fori_loop(0, list_ref[list_ref.shape[0] - 7], start, 0)

    def ready(i, total):
        @pl.when(i < total)
        def _():
            copy(i).wait()

    return ready


def own_kernel(
    dst_ref, code_ref, count_ref, rows_ref, used_ref, features_in_ref, weights_in_ref,
    acc_out_ref, outgoing_ref, early_ref, late_ref,
    own_ref, features_ref, weights_ref, acc_ref, sems,
):
    tiles, size, _ = weights_ref.shape
    loads = [
        pltpu.make_async_copy(features_in_ref, features_ref, sems.at[0]),
        pltpu.make_async_copy(features_in_ref, acc_ref, sems.at[1]),
    ]
    piece = tiles // LOADS
    for i in range(LOADS):
        part = pl.ds(i * piece, piece)
        loads.append(pltpu.make_async_copy(weights_in_ref.at[part], weights_ref.at[part], sems.at[i + 2]))
    for load in loads:
        load.start()
    _, peers, slots = rows_ref.shape
    lists = (own_ref, early_ref, late_ref)

    def sort(t, counts):
        code = code_ref[t]
        stage = code // 65536
        entry = (lax.rem(code, 65536) * 64 + dst_ref[t]) * 256 + t
        for ref, count in zip(lists, counts):
            ref[count] = entry
        return tuple(count + jnp.where(stage == i, 1, 0) for i, count in enumerate(counts))

    counts = lax.fori_loop(0, count_ref[0], sort, (jnp.int32(0),) * 3)
    for ref, count in zip(lists, counts):
        ref[tiles + 1] = count

    loads[0].wait()

    def gather(peer, carry):
        for k in range(slots):
            row = features_ref[pl.ds(rows_ref[0, peer, k], 1), :]
            outgoing_ref[peer, k : k + 1, :] = jnp.where(k < used_ref[0, peer], row, 0.0)
        return carry

    lax.fori_loop(0, peers, gather, 0)

    def source_of(block):
        return features_ref[pl.ds(pl.multiple_of(block * size, size), size), :]

    for load in loads[1:]:
        load.wait()
    add_tiles(own_ref, weights_ref, source_of, acc_ref, lambda i, entry: lax.rem(entry, 256), lambda i, total: None)
    store = pltpu.make_async_copy(acc_ref, acc_out_ref, sems.at[0])
    store.start()
    store.wait()


def own_dense_kernel(
    dst_ref, count_ref, features_in_ref, weights_in_ref, w_self_ref, bias_ref, labels_ref,
    pre_out_ref, aux_out_ref, done_ref,
    features_ref, weights_ref, pre_ref, aux_ref, weight_acc_ref, sems,
):
    done_ref[...] = jnp.zeros_like(done_ref)
    tiles, size, _ = weights_ref.shape
    blocks = weight_acc_ref.shape[0]
    loads = [
        pltpu.make_async_copy(features_in_ref, features_ref, sems.at[0]),
        pltpu.make_async_copy(weights_in_ref, weights_ref, sems.at[1]),
    ]
    for load in loads:
        load.start()
    weight_acc_ref[...] = jnp.zeros_like(weight_acc_ref)
    w_self = split(w_self_ref[...])
    loads[0].wait()

    def dense(i, carry):
        where = pl.ds(pl.multiple_of(i * CHUNK, CHUNK), CHUNK)
        pre_ref[where, :] = dot3(split(features_ref[where, :]), w_self) + bias_ref[...]
        return carry

    lax.fori_loop(0, features_ref.shape[0] // CHUNK, dense, 0, unroll=4)
    stores = [pltpu.make_async_copy(pre_ref, pre_out_ref, sems.at[0])]
    stores[0].start()
    loads[1].wait()

    def add(t, carry):
        weight_acc_ref[dst_ref[t]] += weights_ref[t]
        return carry

    lax.fori_loop(0, count_ref[0], add, 0)

    eye = lax.broadcasted_iota(jnp.int32, (size, size), 0) == lax.broadcasted_iota(jnp.int32, (size, size), 1)
    left = lax.broadcasted_iota(jnp.int32, (size, size), 1) < size // 2

    def columns(block, carry):
        inverse = 1.0 / (1.0 + jnp.sum(weight_acc_ref[block], axis=1, keepdims=True))
        target = 2.0 * labels_ref[pl.ds(block, 1), :].astype(F32) - 1.0
        target = jnp.sum(jnp.where(eye, jnp.broadcast_to(target, eye.shape), 0.0), axis=1, keepdims=True)
        aux_ref[pl.ds(pl.multiple_of(block * size, size), size), :] = jnp.where(left, inverse, target)
        return carry

    lax.fori_loop(0, blocks, columns, 0, unroll=4)
    stores.append(pltpu.make_async_copy(aux_ref, aux_out_ref, sems.at[1]))
    stores[1].start()
    for store in stores:
        store.wait()


def early_kernel(
    list_ref, border_ref, mine_ref, far_ref, other_ref, far_other_ref, acc_in_ref, weights_in_ref, before_ref,
    acc_out_ref, done_ref,
    weights_ref, acc_ref, sources_ref, sems, load_sems,
):
    del before_ref
    done_ref[...] = jnp.zeros_like(done_ref)
    at, copies = 0, [pltpu.make_async_copy(acc_in_ref, acc_ref, load_sems.at[5])]
    for i, part in enumerate((border_ref, mine_ref, far_ref, other_ref, far_other_ref)):
        blocks = part.shape[0]
        copies.append(pltpu.make_async_copy(part, sources_ref.at[pl.ds(at, blocks)], load_sems.at[i]))
        at += blocks
    for copy in copies:
        copy.start()
    ready = fetch_tiles(list_ref, weights_in_ref, weights_ref, sems)
    for copy in copies:
        copy.wait()
    add_tiles(list_ref, weights_ref, lambda i: sources_ref[i], acc_ref, lambda i, entry: i, ready)
    store = pltpu.make_async_copy(acc_ref, acc_out_ref, load_sems.at[0])
    store.start()
    store.wait()


def late_kernel(
    list_ref, place_ref, mine_ref, other_ref, acc_in_ref, weights_in_ref,
    features_in_ref, pre_in_ref, aux_in_ref, w_neigh_ref, w_head_ref, before_ref,
    keep_ref, send_ref,
    weights_ref, acc_ref, features_ref, pre_ref, aux_ref, sources_ref, total_ref, bias_ref, head_ref,
    sems, load_sems, chunk_sems, *, scale,
):
    del before_ref
    verts, width = features_ref.shape
    blocks = mine_ref.shape[0]
    loads = [
        (mine_ref, sources_ref.at[pl.ds(0, blocks)]),
        (other_ref, sources_ref.at[pl.ds(blocks, blocks)]),
        (acc_in_ref, acc_ref),
    ]
    copies = [pltpu.make_async_copy(a, b, load_sems.at[i]) for i, (a, b) in enumerate(loads)]
    for copy in copies:
        copy.start()
    ready = fetch_tiles(list_ref, weights_in_ref, weights_ref, sems)
    chunk_copies = []
    for i in range(verts // CHUNK):
        where = pl.ds(i * CHUNK, CHUNK)
        pairs = ((pre_in_ref, pre_ref), (aux_in_ref, aux_ref), (features_in_ref, features_ref))
        chunk_copies.append(
            [pltpu.make_async_copy(a.at[where], b.at[where], chunk_sems.at[i, j]) for j, (a, b) in enumerate(pairs)]
        )
        for copy in chunk_copies[-1]:
            copy.start()
    total_ref[...] = jnp.zeros_like(total_ref)
    bias_ref[...] = jnp.zeros_like(bias_ref)
    head_ref[...] = jnp.zeros_like(head_ref)
    w_neigh = split(w_neigh_ref[...])
    w_head = w_head_ref[...]
    for copy in copies:
        copy.wait()
    add_tiles(list_ref, weights_ref, lambda i: sources_ref[i], acc_ref, lambda i, entry: i, ready)
    half = aux_ref.shape[1] // 2

    def forward(i):
        where = pl.ds(i * CHUNK, CHUNK)
        columns = aux_ref[where, :]
        mean = split(acc_ref[where, :] * columns[:, 0:1])
        pre = pre_ref[where, :] + dot3(mean, w_neigh)
        sig = jax.nn.sigmoid(pre)
        hidden = pre * sig
        score = jnp.sum(hidden * w_head, axis=1, keepdims=True)
        dscore = (score - columns[:, half : half + 1]) * scale
        dpre = dscore * w_head * (sig * (1.0 + pre * (1.0 - sig)))
        bias_ref[...] += jnp.sum(dpre.reshape(CHUNK // 8, 8, width), axis=0)
        head_ref[...] += jnp.sum((hidden * dscore).reshape(CHUNK // 8, 8, width), axis=0)
        return where, mean, split(dpre)

    for first in range(0, verts // CHUNK, UNROLL):
        for i in range(first, first + UNROLL):
            for copy in chunk_copies[i]:
                copy.wait()
        parts = [forward(i) for i in range(first, first + UNROLL)]
        for where, mean, dpre in parts:
            total_ref[0:width, :] += dot3(split(features_ref[where, :]), dpre, ((0,), (0,)))
            total_ref[width : 2 * width, :] += dot3(mean, dpre, ((0,), (0,)))

    me = place_ref[0]
    rows = 2 * width // 8
    extra = keep_ref.shape[1] - rows
    row_ids = lax.broadcasted_iota(jnp.int32, (extra, width), 0)
    vectors = jnp.where(row_ids == 0, jnp.sum(bias_ref[...], axis=0, keepdims=True), 0.0)
    vectors = jnp.where(row_ids == 1, jnp.sum(head_ref[...], axis=0, keepdims=True), vectors)
    for ref, away in ((keep_ref, 0), (send_ref, 4)):
        for j in range(4):
            piece = me ^ (away + j)
            ref[j, 0:rows, :] = total_ref[pl.ds(pl.multiple_of(piece * rows, rows), rows), :]
            ref[j, rows:, :] = jnp.where(piece == 0, vectors, 0.0)


def finish_kernel(place_ref, mine_ref, other_ref, self_ref, neigh_ref, bias_ref, head_ref):
    me = place_ref[0]
    width = self_ref.shape[1]
    rows = 2 * width // 8
    for ref, away in ((mine_ref, 0), (other_ref, 4)):
        for j in range(4):
            piece = me ^ (away + j)
            part = ref[j, 0:rows, :]
            at = pl.ds(pl.multiple_of(lax.rem(piece, 4) * rows, rows), rows)

            @pl.when(piece < 4)
            def _():
                self_ref[at, :] = part

            @pl.when(piece >= 4)
            def _():
                neigh_ref[at, :] = part

            @pl.when(piece == 0)
            def _():
                bias_ref[...] = ref[j, rows : rows + 1, :]
                head_ref[...] = ref[j, rows + 1 : rows + 2, :]


def keep_in(space, *arrays):
    return [pltpu.with_memory_space_constraint(array, space) for array in arrays]


def shape(*dims, dtype=F32):
    return jax.ShapeDtypeStruct(dims, dtype)


SMEM = pl.BlockSpec(memory_space=pltpu.SMEM)
VMEM = pl.BlockSpec(memory_space=pltpu.VMEM)
ANY = pl.BlockSpec(memory_space=pl.ANY)
HBM = pl.BlockSpec(memory_space=pltpu.HBM)


def on_device(
    peers,
    features,
    w_self,
    w_neigh,
    bias,
    w_head,
    tile_weights,
    tile_dst,
    tile_src,
    tile_count,
    hub_block,
    send_rows,
    send_count,
    labels,
):
    tiles, size, _ = tile_weights.shape
    verts, width = features.shape
    blocks = verts // size
    slots = send_rows.shape[2]
    border_blocks = peers * slots // size
    me = (lax.axis_index("vert") * lax.axis_size("row") + lax.axis_index("row")).astype(jnp.int32)

    bits = peers.bit_length() - 1
    core = 2
    line = [k << (bits - 2) for k in (1, 2, 3)]
    plane = [1 << b for b in range(bits - 2) if 1 << b != core]
    order = (plane[::-1], plane)

    def across(x, mask_of):
        return lax.ppermute(x, AXES, [(i, i ^ mask_of(i)) for i in range(peers)])

    source = tile_src.astype(jnp.int32)
    hub = jnp.clip(source - blocks - border_blocks, 0, peers - 1)
    apart = hub ^ me
    place_in_line = apart >> (bits - 2)
    sender_core = (hub >> 1) & 1
    steps = len(plane)

    def differs(s):
        return jnp.where(sender_core == 0, apart & order[0][s], apart & order[1][s]) != 0

    held_blocks, far_blocks = peers // 4, peers // 8
    index = place_in_line
    for s in range(steps - 1):
        index = index + jnp.where(differs(s), 4 << s, 0)
    through = differs(steps - 1)
    late = through & (index >= far_blocks)
    early_code = 65536 + border_blocks + index + jnp.where(through, held_blocks, 0)
    early_code = early_code + jnp.where((apart & core) != 0, held_blocks + far_blocks, 0)
    late_code = 2 * 65536 + index - far_blocks + jnp.where((apart & core) != 0, far_blocks, 0)
    code = jnp.where(late, late_code, early_code)
    code = jnp.where(source < blocks + border_blocks, 65536 + source - blocks, code)
    code = jnp.where(source < blocks, source, code)

    mine = lax.dynamic_slice_in_dim(features, hub_block[0] * size, size, 0)[None]
    held = jnp.concatenate([mine] + [across(mine, lambda i, m=m: m) for m in line], 0)

    features, tile_weights = keep_in(pltpu.HBM, features, tile_weights)
    acc, outgoing, early_list, late_list = pl.pallas_call(
        own_kernel,
        out_shape=(
            pltpu.HBM((verts, width), F32),
            shape(peers, slots, width),
            shape(tiles + 8, dtype=jnp.int32),
            shape(tiles + 8, dtype=jnp.int32),
        ),
        in_specs=[SMEM] * 5 + [HBM, HBM],
        out_specs=(HBM, VMEM, SMEM, SMEM),
        scratch_shapes=[
            pltpu.SMEM((tiles + 8,), jnp.int32),
            pltpu.VMEM((verts, width), F32),
            pltpu.VMEM((tiles, size, size), F32),
            pltpu.VMEM((verts, width), F32),
            pltpu.SemaphoreType.DMA((LOADS + 2,)),
        ],
        compiler_params=pltpu.CompilerParams(vmem_limit_bytes=VMEM_BYTES),
        cost_estimate=COST,
        name="own_tiles",
    )(tile_dst, code, tile_count, send_rows, send_count, features, tile_weights)
    held, outgoing = lax.optimization_barrier((held, outgoing))

    pre, aux, done = pl.pallas_call(
        own_dense_kernel,
        out_shape=(pltpu.HBM((verts, width), F32), pltpu.HBM((verts, size), F32), shape(8, size)),
        in_specs=[SMEM] * 2 + [HBM, HBM, VMEM, VMEM, VMEM],
        out_specs=(HBM, HBM, VMEM),
        scratch_shapes=[
            pltpu.VMEM((verts, width), F32),
            pltpu.VMEM((tiles, size, size), F32),
            pltpu.VMEM((verts, width), F32),
            pltpu.VMEM((verts, size), F32),
            pltpu.VMEM((blocks, size, size), F32),
            pltpu.SemaphoreType.DMA((2,)),
        ],
        compiler_params=pltpu.CompilerParams(vmem_limit_bytes=VMEM_BYTES),
        cost_estimate=COST,
        name="own_dense",
    )(
        tile_dst, tile_count, features, tile_weights, w_self, bias.reshape(1, width),
        labels.reshape(blocks, size),
    )

    incoming = lax.all_to_all(outgoing, AXES, split_axis=0, concat_axis=0, tiled=True)
    border = incoming.reshape(border_blocks, size, width)

    for s in range(steps - 1):
        near = held
        held = jnp.concatenate([held, across(held, lambda i, s=s: order[(i >> 1) & 1][s])], 0)
    far_near = across(near, lambda i: order[(i >> 1) & 1][steps - 1])
    held, far_near, border, done = lax.optimization_barrier((held, far_near, border, done))
    far = across(held[far_blocks:], lambda i: order[(i >> 1) & 1][steps - 1])
    held_other = across(held, lambda i: core)
    far_near_other = across(far_near, lambda i: core)

    acc, done = pl.pallas_call(
        early_kernel,
        out_shape=(pltpu.HBM((verts, width), F32), shape(8, size)),
        in_specs=[SMEM] + [ANY] * 5 + [HBM, HBM, ANY],
        out_specs=(HBM, VMEM),
        scratch_shapes=[
            pltpu.VMEM((tiles, size, size), F32),
            pltpu.VMEM((verts, width), F32),
            pltpu.VMEM((border_blocks + 2 * (held_blocks + far_blocks), size, width), F32),
            pltpu.SemaphoreType.DMA((tiles,)),
            pltpu.SemaphoreType.DMA((6,)),
        ],
        compiler_params=pltpu.CompilerParams(vmem_limit_bytes=VMEM_BYTES),
        cost_estimate=COST,
        name="early_tiles",
    )(
        early_list, border, held, far_near, held_other, far_near_other,
        *keep_in(pltpu.HBM, acc), tile_weights, done,
    )
    far, done = lax.optimization_barrier((far, done))
    far_other = across(far, lambda i: core)

    place = ((me >> 1) & 1) * 4 + ((me >> 2) & 1) * 2 + (me & 1)
    place = place.reshape(1)
    piece_rows = 2 * width // 8 + 8
    keep, send = pl.pallas_call(
        functools.partial(late_kernel, scale=1.0 / math.sqrt(verts * peers)),
        out_shape=(shape(4, piece_rows, width), shape(4, piece_rows, width)),
        in_specs=[SMEM, SMEM, ANY, ANY] + [HBM] * 5 + [VMEM, VMEM, ANY],
        out_specs=(VMEM, VMEM),
        scratch_shapes=[
            pltpu.VMEM((tiles, size, size), F32),
            pltpu.VMEM((verts, width), F32),
            pltpu.VMEM((verts, width), F32),
            pltpu.VMEM((verts, width), F32),
            pltpu.VMEM((verts, size), F32),
            pltpu.VMEM((2 * far_blocks, size, width), F32),
            pltpu.VMEM((2 * width, width), F32),
            pltpu.VMEM((8, width), F32),
            pltpu.VMEM((8, width), F32),
            pltpu.SemaphoreType.DMA((tiles,)),
            pltpu.SemaphoreType.DMA((3,)),
            pltpu.SemaphoreType.DMA((verts // CHUNK, 3)),
        ],
        compiler_params=pltpu.CompilerParams(vmem_limit_bytes=VMEM_BYTES),
        cost_estimate=COST,
        name="late_tiles_and_gradients",
    )(
        late_list, place, far, far_other,
        *keep_in(pltpu.HBM, acc, tile_weights, features, pre, aux),
        w_neigh, w_head.reshape(1, width), done,
    )

    held = keep + across(send, lambda i: core)
    reach = (0, 1, 4, 5)
    got = [held[0]] + [across(held[j], lambda i, j=j: reach[j]) for j in (1, 2, 3)]
    total = (got[0] + got[1]) + (got[2] + got[3])
    for low in range(3, bits, 2):
        masks = [1 << low] if low + 1 == bits else [k << low for k in (1, 2, 3)]
        more = [across(total, lambda i, m=m: m) for m in masks]
        total = total + more[0] if len(more) == 1 else (total + more[0]) + (more[1] + more[2])
    mine = jnp.stack([total] + [across(total, lambda i, j=j: reach[j]) for j in (1, 2, 3)])
    other = across(mine, lambda i: core)
    grad_self, grad_neigh, grad_bias, grad_head = pl.pallas_call(
        finish_kernel,
        out_shape=(shape(width, width), shape(width, width), shape(1, width), shape(1, width)),
        in_specs=[SMEM, VMEM, VMEM],
        out_specs=(VMEM, VMEM, VMEM, VMEM),
        name="assemble",
    )(place, mine, other)
    return (grad_self, grad_neigh, grad_bias.reshape(width), grad_head.reshape(width))


def solution(mesh):
    peers = math.prod(mesh.shape.values())
    in_specs = (
        P(AXES, None),
        P(),
        P(),
        P(),
        P(),
        P(AXES, None, None),
        P(AXES),
        P(AXES),
        P(AXES),
        P(AXES),
        P(AXES, None, None),
        P(AXES, None),
        P(AXES),
    )
    out_specs = (P(), P(), P(), P())
    return jax.shard_map(
        functools.partial(on_device, peers),
        mesh=mesh,
        in_specs=in_specs,
        out_specs=out_specs,
        check_vma=False,
    )
```

```python
import functools
import math

import jax
import jax.numpy as jnp
from jax import lax
from jax.experimental import pallas as pl
from jax.experimental.pallas import tpu as pltpu
from jax.sharding import PartitionSpec as P

AXES = ("vert", "row")
F32 = jnp.float32
BF16 = jnp.bfloat16
GROUP = 8
CHUNK = 512
COST = pl.CostEstimate(flops=1_000_000, bytes_accessed=100_000, transcendentals=0)
UNROLL = 4
VMEM_BYTES = 44 * 1024 * 1024


def split(x):
    hi = x.astype(BF16)
    return hi, (x - hi.astype(F32)).astype(BF16)


def dot(a, b, contract=((1,), (0,))):
    return lax.dot_general(a, b, (contract, ((), ())), preferred_element_type=F32)


def dot3(a, b, contract=((1,), (0,))):
    (a_hi, a_lo), (b_hi, b_lo) = a, b
    return dot(a_hi, b_hi, contract) + dot(a_hi, b_lo, contract) + dot(a_lo, b_hi, contract)


def tile_product(weights, source):
    w_hi, w_lo = split(weights)
    s_hi, s_lo = split(source)
    wide = jnp.concatenate([w_hi, w_hi], 1)
    tall = jnp.concatenate([s_hi, s_lo], 0)
    return dot(wide, tall) + dot(w_lo, s_hi)


def add_tiles(list_ref, weights_ref, source_of, acc_ref, weight_acc_ref, ready):
    size = weights_ref.shape[1]
    total = list_ref[list_ref.shape[0] - 7]

    def step(group, carry):
        ready(group)
        at = [group * GROUP + k for k in range(GROUP)]
        entries = [list_ref[jnp.minimum(i, total - 1)] for i in at]
        products = [
            tile_product(weights_ref[i], source_of(entry >> 14))
            for i, entry in zip(at, entries)
        ]
        for i, entry, product in zip(at, entries, products):
            block = (entry >> 8) & 63
            where = pl.ds(pl.multiple_of(block * size, size), size)
            acc_ref[where, :] += jnp.where(i < total, product, 0.0)
            weight_acc_ref[block] += jnp.where(i < total, weights_ref[i], 0.0)
        return carry

    lax.fori_loop(0, (total + GROUP - 1) // GROUP, step, 0)


def row_sums(weight_acc_ref, sums_ref):
    blocks, size, _ = weight_acc_ref.shape

    def step(block, carry):
        column = jnp.sum(weight_acc_ref[block], axis=1, keepdims=True)
        sums_ref[pl.ds(block, 1), :] = jnp.sum(jnp.where(diagonal(size), column, 0.0), axis=0, keepdims=True)
        return carry

    lax.fori_loop(0, blocks, step, 0, unroll=4)


def diagonal(size):
    at = lambda axis: lax.broadcasted_iota(jnp.int32, (size, size), axis)
    return at(0) == at(1)


def as_columns(rows):
    size = rows.shape[1]
    parts = [
        jnp.sum(jnp.where(diagonal(size), rows[i : i + 1, :], 0.0), axis=1, keepdims=True)
        for i in range(rows.shape[0])
    ]
    return jnp.concatenate(parts, 0)


def fetch_tiles(list_ref, weights_in_ref, weights_ref, sems):
    total = list_ref[list_ref.shape[0] - 7]

    def start(group, carry):
        for k in range(GROUP):
            i = group * GROUP + k
            tile = list_ref[jnp.minimum(i, total - 1)] & 255
            pltpu.make_async_copy(weights_in_ref.at[tile], weights_ref.at[i], sems.at[group]).start()
        return carry

    lax.fori_loop(0, (total + GROUP - 1) // GROUP, start, 0)

    def ready(group):
        part = weights_ref.at[pl.ds(pl.multiple_of(group * GROUP, GROUP), GROUP)]
        pltpu.make_async_copy(weights_in_ref.at[pl.ds(0, GROUP)], part, sems.at[group]).wait()

    return ready


def prepare_kernel(
    plan_ref, rows_ref, count_ref, features_in_ref,
    outgoing_ref, own_ref, early_ref, late_ref,
    features_ref, load_sems,
):
    load = pltpu.make_async_copy(features_in_ref, features_ref, load_sems.at[0])
    load.start()
    tiles = plan_ref.shape[0]
    peers, slots, _ = outgoing_ref.shape
    lists = (own_ref, early_ref, late_ref)

    def sort(t, counts):
        plan = plan_ref[t]
        stage = plan >> 28
        entry = (plan & ((1 << 28) - 1)) | t
        for ref, count in zip(lists, counts):
            ref[count] = entry
        return tuple(count + (stage == i).astype(jnp.int32) for i, count in enumerate(counts))

    counts = lax.fori_loop(0, count_ref[0], sort, (jnp.int32(0),) * 3)
    for ref, count in zip(lists, counts):
        ref[tiles + 1] = count
    load.wait()

    def gather(peer, carry):
        for k in range(slots):
            at = rows_ref[peer * slots + k]
            row = features_ref[pl.ds(jnp.maximum(at, 0), 1), :]
            outgoing_ref[peer, k : k + 1, :] = jnp.where(at >= 0, row, 0.0)
        return carry

    lax.fori_loop(0, peers, gather, 0)


def own_kernel(
    list_ref, features_in_ref, weights_in_ref,
    acc_out_ref, sums_ref,
    features_ref, weights_ref, acc_ref, weight_acc_ref, sems, load_sems,
):
    size = weights_ref.shape[1]
    load = pltpu.make_async_copy(features_in_ref, features_ref, load_sems.at[0])
    load.start()
    ready = fetch_tiles(list_ref, weights_in_ref, weights_ref, sems)
    acc_ref[...] = jnp.zeros_like(acc_ref)
    weight_acc_ref[...] = jnp.zeros_like(weight_acc_ref)
    load.wait()

    def source_of(block):
        return features_ref[pl.ds(pl.multiple_of(block * size, size), size), :]

    add_tiles(list_ref, weights_ref, source_of, acc_ref, weight_acc_ref, ready)
    store = pltpu.make_async_copy(acc_ref, acc_out_ref, load_sems.at[0])
    store.start()
    row_sums(weight_acc_ref, sums_ref)
    store.wait()


def early_kernel(
    list_ref, border_ref, mine_ref, far_ref, other_ref, far_other_ref, weights_in_ref,
    acc_out_ref, sums_ref,
    weights_ref, acc_ref, weight_acc_ref, sources_ref, sems, load_sems,
):
    at, copies = 0, []
    for i, part in enumerate((border_ref, mine_ref, far_ref, other_ref, far_other_ref)):
        blocks = part.shape[0]
        copies.append(pltpu.make_async_copy(part, sources_ref.at[pl.ds(at, blocks)], load_sems.at[i]))
        at += blocks
    for copy in copies:
        copy.start()
    ready = fetch_tiles(list_ref, weights_in_ref, weights_ref, sems)
    acc_ref[...] = jnp.zeros_like(acc_ref)
    weight_acc_ref[...] = jnp.zeros_like(weight_acc_ref)
    for copy in copies:
        copy.wait()
    add_tiles(list_ref, weights_ref, lambda i: sources_ref[i], acc_ref, weight_acc_ref, ready)
    store = pltpu.make_async_copy(acc_ref, acc_out_ref, load_sems.at[0])
    store.start()
    row_sums(weight_acc_ref, sums_ref)
    store.wait()


def late_kernel(
    list_ref, place_ref, mine_ref, other_ref, own_in_ref, early_in_ref, weights_in_ref, features_in_ref,
    own_sums_ref, early_sums_ref, labels_ref, w_self_ref, w_neigh_ref, bias_in_ref, w_head_ref,
    keep_ref, send_ref,
    weights_ref, weight_acc_ref, acc_ref, own_ref, early_ref, features_ref, sources_ref, sums_ref, total_ref, bias_ref, head_ref,
    sems, load_sems, chunk_sems, *, scale,
):
    verts, width = features_ref.shape
    size = weights_ref.shape[1]
    blocks = mine_ref.shape[0]
    loads = [
        (mine_ref, sources_ref.at[pl.ds(0, blocks)]),
        (other_ref, sources_ref.at[pl.ds(blocks, blocks)]),
    ]
    copies = [pltpu.make_async_copy(a, b, load_sems.at[i]) for i, (a, b) in enumerate(loads)]
    for copy in copies:
        copy.start()
    ready = fetch_tiles(list_ref, weights_in_ref, weights_ref, sems)
    chunk_copies = []
    for i in range(verts // CHUNK):
        where = pl.ds(i * CHUNK, CHUNK)
        pairs = ((own_in_ref, own_ref), (early_in_ref, early_ref), (features_in_ref, features_ref))
        chunk_copies.append(
            [pltpu.make_async_copy(a.at[where], b.at[where], chunk_sems.at[i, j]) for j, (a, b) in enumerate(pairs)]
        )
        for copy in chunk_copies[-1]:
            copy.start()
    acc_ref[...] = jnp.zeros_like(acc_ref)
    weight_acc_ref[...] = jnp.zeros_like(weight_acc_ref)
    total_ref[...] = jnp.zeros_like(total_ref)
    bias_ref[...] = jnp.zeros_like(bias_ref)
    head_ref[...] = jnp.zeros_like(head_ref)
    w_self = split(w_self_ref[...])
    w_neigh = split(w_neigh_ref[...])
    w_head = w_head_ref[...]
    for copy in copies:
        copy.wait()
    add_tiles(list_ref, weights_ref, lambda i: sources_ref[i], acc_ref, weight_acc_ref, ready)
    row_sums(weight_acc_ref, sums_ref)
    inverse = 1.0 / (1.0 + (own_sums_ref[...] + early_sums_ref[...] + sums_ref[...]))
    target = 2.0 * labels_ref[...].astype(F32) - 1.0
    step = CHUNK // size

    def forward(i):
        where = pl.ds(i * CHUNK, CHUNK)
        own = features_ref[where, :]
        mean = (own + (acc_ref[where, :] + own_ref[where, :] + early_ref[where, :])) * as_columns(inverse[i * step : (i + 1) * step, :])
        own, mean = split(own), split(mean)
        pre = dot3(own, w_self) + dot3(mean, w_neigh) + bias_in_ref[...]
        sig = jax.nn.sigmoid(pre)
        hidden = pre * sig
        score = jnp.sum(hidden * w_head, axis=1, keepdims=True)
        dscore = (score - as_columns(target[i * step : (i + 1) * step, :])) * scale
        dpre = dscore * w_head * (sig * (1.0 + pre * (1.0 - sig)))
        bias_ref[...] += jnp.sum(dpre.reshape(CHUNK // 8, 8, width), axis=0)
        head_ref[...] += jnp.sum((hidden * dscore).reshape(CHUNK // 8, 8, width), axis=0)
        return own, mean, split(dpre)

    def backward(own, mean, dpre):
        total_ref[0:width, :] += dot3(own, dpre, ((0,), (0,)))
        total_ref[width : 2 * width, :] += dot3(mean, dpre, ((0,), (0,)))

    for first in range(0, verts // CHUNK, UNROLL):
        for i in range(first, first + UNROLL):
            for copy in chunk_copies[i]:
                copy.wait()
        for parts in [forward(i) for i in range(first, first + UNROLL)]:
            backward(*parts)

    me = place_ref[0]
    rows = 2 * width // 8
    extra = keep_ref.shape[1] - rows
    row_ids = lax.broadcasted_iota(jnp.int32, (extra, width), 0)
    vectors = jnp.where(row_ids == 0, jnp.sum(bias_ref[...], axis=0, keepdims=True), 0.0)
    vectors = jnp.where(row_ids == 1, jnp.sum(head_ref[...], axis=0, keepdims=True), vectors)
    for ref, away in ((keep_ref, 0), (send_ref, 4)):
        for j in range(4):
            piece = me ^ (away + j)
            ref[j, 0:rows, :] = total_ref[pl.ds(pl.multiple_of(piece * rows, rows), rows), :]
            ref[j, rows:, :] = jnp.where(piece == 0, vectors, 0.0)


def finish_kernel(place_ref, mine_ref, other_ref, self_ref, neigh_ref, bias_ref, head_ref):
    me = place_ref[0]
    width = self_ref.shape[1]
    rows = 2 * width // 8
    for ref, away in ((mine_ref, 0), (other_ref, 4)):
        for j in range(4):
            piece = me ^ (away + j)
            part = ref[j, 0:rows, :]
            at = pl.ds(pl.multiple_of(lax.rem(piece, 4) * rows, rows), rows)

            @pl.when(piece < 4)
            def _():
                self_ref[at, :] = part

            @pl.when(piece >= 4)
            def _():
                neigh_ref[at, :] = part

            @pl.when(piece == 0)
            def _():
                bias_ref[...] = ref[j, rows : rows + 1, :]
                head_ref[...] = ref[j, rows + 1 : rows + 2, :]


def keep_in(space, *arrays):
    return [pltpu.with_memory_space_constraint(array, space) for array in arrays]


def shape(*dims, dtype=F32):
    return jax.ShapeDtypeStruct(dims, dtype)


SMEM = pl.BlockSpec(memory_space=pltpu.SMEM)
VMEM = pl.BlockSpec(memory_space=pltpu.VMEM)
ANY = pl.BlockSpec(memory_space=pl.ANY)
HBM = pl.BlockSpec(memory_space=pltpu.HBM)


def on_device(
    peers,
    features,
    w_self,
    w_neigh,
    bias,
    w_head,
    tile_weights,
    tile_dst,
    tile_src,
    tile_count,
    hub_block,
    send_rows,
    send_count,
    labels,
):
    tiles, size, _ = tile_weights.shape
    verts, width = features.shape
    blocks = verts // size
    slots = send_rows.shape[2]
    border_blocks = peers * slots // size
    me = (lax.axis_index("vert") * lax.axis_size("row") + lax.axis_index("row")).astype(jnp.int32)

    bits = peers.bit_length() - 1
    core = 2
    line = [k << (bits - 2) for k in (1, 2, 3)]
    plane = [1 << b for b in range(bits - 2) if 1 << b != core]
    order = (plane[::-1], plane)

    def across(x, mask_of):
        return lax.ppermute(x, AXES, [(i, i ^ mask_of(i)) for i in range(peers)])

    source = tile_src.astype(jnp.int32)
    hub = jnp.clip(source - blocks - border_blocks, 0, peers - 1)
    apart = hub ^ me
    place_in_line = apart >> (bits - 2)
    sender_core = (hub >> 1) & 1
    steps = len(plane)

    def differs(s):
        return jnp.where(sender_core == 0, apart & order[0][s], apart & order[1][s]) != 0

    held_blocks, far_blocks = peers // 4, peers // 8
    index = place_in_line
    for s in range(steps - 1):
        index = index + jnp.where(differs(s), 4 << s, 0)
    through = differs(steps - 1)
    late = through & (index >= far_blocks)
    early_slot = border_blocks + index + jnp.where(through, held_blocks, 0)
    early_slot = early_slot + jnp.where((apart & core) != 0, held_blocks + far_blocks, 0)
    late_slot = index - far_blocks + jnp.where((apart & core) != 0, far_blocks, 0)
    stage = jnp.where(late, 2, 1)
    slot = jnp.where(late, late_slot, early_slot)
    at_border = source < blocks + border_blocks
    stage = jnp.where(source < blocks, 0, jnp.where(at_border, 1, stage))
    slot = jnp.where(source < blocks, source, jnp.where(at_border, source - blocks, slot))
    plan = (stage << 28) | (slot << 14) | (tile_dst << 8)
    alive = jnp.arange(slots, dtype=jnp.int32)[None, :] < send_count[0][:, None]
    listed = jnp.where(alive, send_rows[0], -1).reshape(-1)

    mine = lax.dynamic_slice_in_dim(features, hub_block[0] * size, size, 0)[None]
    held = jnp.concatenate([mine] + [across(mine, lambda i, m=m: m) for m in line], 0)

    features, tile_weights = keep_in(pltpu.HBM, features, tile_weights)
    index_list = shape(tiles + 8, dtype=jnp.int32)
    outgoing, own_list, early_list, late_list = pl.pallas_call(
        prepare_kernel,
        out_shape=(shape(peers, slots, width),) + (index_list,) * 3,
        in_specs=[SMEM] * 3 + [HBM],
        out_specs=(VMEM, SMEM, SMEM, SMEM),
        scratch_shapes=[pltpu.VMEM((verts, width), F32), pltpu.SemaphoreType.DMA((1,))],
        compiler_params=pltpu.CompilerParams(vmem_limit_bytes=VMEM_BYTES),
        cost_estimate=COST,
        name="prepare",
    )(*keep_in(pltpu.HBM, plan, listed), tile_count, features)
    held, outgoing, own_list = lax.optimization_barrier((held, outgoing, own_list))

    own_acc, own_sums = pl.pallas_call(
        own_kernel,
        out_shape=(pltpu.HBM((verts, width), F32), shape(blocks, size)),
        in_specs=[SMEM, HBM, HBM],
        out_specs=(HBM, VMEM),
        scratch_shapes=[
            pltpu.VMEM((verts, width), F32),
            pltpu.VMEM((tiles, size, size), F32),
            pltpu.VMEM((verts, width), F32),
            pltpu.VMEM((blocks, size, size), F32),
            pltpu.SemaphoreType.DMA((tiles // GROUP,)),
            pltpu.SemaphoreType.DMA((1,)),
        ],
        compiler_params=pltpu.CompilerParams(vmem_limit_bytes=VMEM_BYTES),
        cost_estimate=COST,
        name="own_tiles",
    )(own_list, features, tile_weights)

    incoming = lax.all_to_all(outgoing, AXES, split_axis=0, concat_axis=0, tiled=True)
    border = incoming.reshape(border_blocks, size, width)

    for s in range(steps - 1):
        near = held
        held = jnp.concatenate([held, across(held, lambda i, s=s: order[(i >> 1) & 1][s])], 0)
    far_near = across(near, lambda i: order[(i >> 1) & 1][steps - 1])
    held, far_near, border, own_sums = lax.optimization_barrier((held, far_near, border, own_sums))
    far = across(held[far_blocks:], lambda i: order[(i >> 1) & 1][steps - 1])
    held_other = across(held, lambda i: core)
    far_near_other = across(far_near, lambda i: core)

    early_acc, early_sums = pl.pallas_call(
        early_kernel,
        out_shape=(pltpu.HBM((verts, width), F32), shape(blocks, size)),
        in_specs=[SMEM] + [ANY] * 5 + [HBM],
        out_specs=(HBM, VMEM),
        scratch_shapes=[
            pltpu.VMEM((tiles, size, size), F32),
            pltpu.VMEM((verts, width), F32),
            pltpu.VMEM((blocks, size, size), F32),
            pltpu.VMEM((border_blocks + 2 * (held_blocks + far_blocks), size, width), F32),
            pltpu.SemaphoreType.DMA((tiles // GROUP,)),
            pltpu.SemaphoreType.DMA((5,)),
        ],
        compiler_params=pltpu.CompilerParams(vmem_limit_bytes=VMEM_BYTES),
        cost_estimate=COST,
        name="early_tiles",
    )(early_list, border, held, far_near, held_other, far_near_other, tile_weights)
    far, early_sums = lax.optimization_barrier((far, early_sums))
    far_other = across(far, lambda i: core)

    place = ((me >> 1) & 1) * 4 + ((me >> 2) & 1) * 2 + (me & 1)
    place = place.reshape(1)
    piece_rows = 2 * width // 8 + 8
    keep, send = pl.pallas_call(
        functools.partial(late_kernel, scale=1.0 / math.sqrt(verts * peers)),
        out_shape=(shape(4, piece_rows, width), shape(4, piece_rows, width)),
        in_specs=[SMEM, SMEM, ANY, ANY] + [HBM] * 4 + [VMEM] * 7,
        out_specs=(VMEM, VMEM),
        scratch_shapes=[
            pltpu.VMEM((tiles, size, size), F32),
            pltpu.VMEM((blocks, size, size), F32),
            pltpu.VMEM((verts, width), F32),
            pltpu.VMEM((verts, width), F32),
            pltpu.VMEM((verts, width), F32),
            pltpu.VMEM((verts, width), F32),
            pltpu.VMEM((2 * far_blocks, size, width), F32),
            pltpu.VMEM((blocks, size), F32),
            pltpu.VMEM((2 * width, width), F32),
            pltpu.VMEM((8, width), F32),
            pltpu.VMEM((8, width), F32),
            pltpu.SemaphoreType.DMA((tiles // GROUP,)),
            pltpu.SemaphoreType.DMA((2,)),
            pltpu.SemaphoreType.DMA((verts // CHUNK, 3)),
        ],
        compiler_params=pltpu.CompilerParams(vmem_limit_bytes=VMEM_BYTES),
        cost_estimate=COST,
        name="late_tiles_and_gradients",
    )(
        late_list, place, far, far_other,
        *keep_in(pltpu.HBM, own_acc, early_acc), tile_weights, features,
        own_sums, early_sums, labels.reshape(blocks, size),
        w_self, w_neigh, bias.reshape(1, width), w_head.reshape(1, width),
    )

    held = keep + across(send, lambda i: core)
    reach = (0, 1, 4, 5)
    got = [held[0]] + [across(held[j], lambda i, j=j: reach[j]) for j in (1, 2, 3)]
    total = (got[0] + got[1]) + (got[2] + got[3])
    for low in range(3, bits, 2):
        masks = [1 << low] if low + 1 == bits else [k << low for k in (1, 2, 3)]
        more = [across(total, lambda i, m=m: m) for m in masks]
        total = total + more[0] if len(more) == 1 else (total + more[0]) + (more[1] + more[2])
    mine = jnp.stack([total] + [across(total, lambda i, j=j: reach[j]) for j in (1, 2, 3)])
    other = across(mine, lambda i: core)
    grad_self, grad_neigh, grad_bias, grad_head = pl.pallas_call(
        finish_kernel,
        out_shape=(shape(width, width), shape(width, width), shape(1, width), shape(1, width)),
        in_specs=[SMEM, VMEM, VMEM],
        out_specs=(VMEM, VMEM, VMEM, VMEM),
        name="assemble",
    )(place, *keep_in(pltpu.VMEM, mine, other))
    return (grad_self, grad_neigh, grad_bias.reshape(width), grad_head.reshape(width))


def solution(mesh):
    peers = math.prod(mesh.shape.values())
    in_specs = (
        P(AXES, None),
        P(),
        P(),
        P(),
        P(),
        P(AXES, None, None),
        P(AXES),
        P(AXES),
        P(AXES),
        P(AXES),
        P(AXES, None, None),
        P(AXES, None),
        P(AXES),
    )
    out_specs = (P(), P(), P(), P())
    return jax.shard_map(
        functools.partial(on_device, peers),
        mesh=mesh,
        in_specs=in_specs,
        out_specs=out_specs,
        check_vma=False,
    )
```

```python
import functools
import math

import jax
import jax.numpy as jnp
from jax import lax
from jax.experimental import pallas as pl
from jax.experimental.pallas import tpu as pltpu
from jax.sharding import PartitionSpec as P

AXES = ("vert", "row")
F32 = jnp.float32
BF16 = jnp.bfloat16
GROUP = 8
CHUNK = 512
COST = pl.CostEstimate(flops=1_000_000, bytes_accessed=100_000, transcendentals=0)
UNROLL = 4
VMEM_BYTES = 44 * 1024 * 1024


def split(x):
    hi = x.astype(BF16)
    return hi, (x - hi.astype(F32)).astype(BF16)


def dot(a, b, contract=((1,), (0,))):
    return lax.dot_general(a, b, (contract, ((), ())), preferred_element_type=F32)


def dot3(a, b, contract=((1,), (0,))):
    (a_hi, a_lo), (b_hi, b_lo) = a, b
    return dot(a_hi, b_hi, contract) + dot(a_hi, b_lo, contract) + dot(a_lo, b_hi, contract)


def tile_product(weights, source):
    w_hi, w_lo = split(weights)
    s_hi, s_lo = split(source)
    wide = jnp.concatenate([w_hi, w_hi], 1)
    tall = jnp.concatenate([s_hi, s_lo], 0)
    return dot(wide, tall) + dot(w_lo, s_hi)


def listed_at(list_ref, i):
    tiles = list_ref.shape[0] - 8
    total, lower = list_ref[tiles + 1], list_ref[tiles + 2]
    i = jnp.minimum(i, total - 1)
    return list_ref[i + jnp.where(i >= lower, tiles - total, 0)]


def add_tiles(list_ref, weights_ref, source_of, acc_ref, weight_acc_ref, ready, lower_done=None):
    size = weights_ref.shape[1]
    total = list_ref[list_ref.shape[0] - 7]

    def step(group, carry):
        ready(group)
        at = [group * GROUP + k for k in range(GROUP)]
        entries = [listed_at(list_ref, i) for i in at]
        products = [
            tile_product(weights_ref[i], source_of(entry >> 14))
            for i, entry in zip(at, entries)
        ]
        for i, entry, product in zip(at, entries, products):
            block = (entry >> 8) & 63
            where = pl.ds(pl.multiple_of(block * size, size), size)
            acc_ref[where, :] += jnp.where(i < total, product, 0.0)
            weight_acc_ref[block] += jnp.where(i < total, weights_ref[i], 0.0)
        return carry

    groups = (total + GROUP - 1) // GROUP
    if lower_done is None:
        lax.fori_loop(0, groups, step, 0)
    else:
        lower = (list_ref[list_ref.shape[0] - 6] + GROUP - 1) // GROUP
        lax.fori_loop(0, lower, step, 0)
        lower_done()
        lax.fori_loop(lower, groups, step, 0)


def halves_out(acc_ref, out_ref, sems):
    half = acc_ref.shape[0] // 2
    parts = [pl.ds(i * half, half) for i in range(2)]
    return [pltpu.make_async_copy(acc_ref.at[part], out_ref.at[part], sems.at[i]) for i, part in enumerate(parts)]


def row_sums(weight_acc_ref, sums_ref):
    blocks, size, _ = weight_acc_ref.shape

    def step(block, carry):
        column = jnp.sum(weight_acc_ref[block], axis=1, keepdims=True)
        sums_ref[pl.ds(block, 1), :] = jnp.sum(jnp.where(diagonal(size), column, 0.0), axis=0, keepdims=True)
        return carry

    lax.fori_loop(0, blocks, step, 0, unroll=4)


def diagonal(size):
    at = lambda axis: lax.broadcasted_iota(jnp.int32, (size, size), axis)
    return at(0) == at(1)


def as_columns(rows):
    size = rows.shape[1]
    parts = [
        jnp.sum(jnp.where(diagonal(size), rows[i : i + 1, :], 0.0), axis=1, keepdims=True)
        for i in range(rows.shape[0])
    ]
    return jnp.concatenate(parts, 0)


def fetch_tiles(list_ref, weights_in_ref, weights_ref, sems):
    total = list_ref[list_ref.shape[0] - 7]

    def start(group, carry):
        for k in range(GROUP):
            i = group * GROUP + k
            tile = listed_at(list_ref, i) & 255
            pltpu.make_async_copy(weights_in_ref.at[tile], weights_ref.at[i], sems.at[group]).start()
        return carry

    lax.fori_loop(0, (total + GROUP - 1) // GROUP, start, 0)

    def ready(group):
        part = weights_ref.at[pl.ds(pl.multiple_of(group * GROUP, GROUP), GROUP)]
        pltpu.make_async_copy(weights_in_ref.at[pl.ds(0, GROUP)], part, sems.at[group]).wait()

    return ready


def prepare_kernel(
    plan_ref, rows_ref, count_ref, features_in_ref,
    outgoing_ref, own_ref, early_ref, late_ref,
    features_ref, load_sems, *, size,
):
    load = pltpu.make_async_copy(features_in_ref, features_ref, load_sems.at[0])
    load.start()
    tiles = plan_ref.shape[0]
    peers, slots, _ = outgoing_ref.shape
    lists = (own_ref, early_ref, late_ref)

    lower_blocks = features_ref.shape[0] // (2 * size)

    def sort(t, counts):
        plan = plan_ref[t]
        stage = plan >> 28
        entry = (plan & ((1 << 28) - 1)) | t
        upper = (((plan >> 8) & 63) >= lower_blocks).astype(jnp.int32)
        after = []
        for i, (ref, (low, high)) in enumerate(zip(lists, counts)):
            ref[jnp.where(upper == 1, tiles - 1 - high, low)] = entry
            mine = (stage == i).astype(jnp.int32)
            after.append((low + (mine & (1 - upper)), high + (mine & upper)))
        return tuple(after)

    counts = lax.fori_loop(0, count_ref[0], sort, ((jnp.int32(0), jnp.int32(0)),) * 3)
    for ref, (low, high) in zip(lists, counts):
        ref[tiles + 1] = low + high
        ref[tiles + 2] = low
    load.wait()

    def gather(peer, carry):
        for k in range(slots):
            at = rows_ref[peer * slots + k]
            row = features_ref[pl.ds(jnp.maximum(at, 0), 1), :]
            outgoing_ref[peer, k : k + 1, :] = jnp.where(at >= 0, row, 0.0)
        return carry

    lax.fori_loop(0, peers, gather, 0)


def own_kernel(
    list_ref, features_in_ref, weights_in_ref,
    acc_out_ref, sums_ref,
    features_ref, weights_ref, acc_ref, weight_acc_ref, sems, load_sems,
):
    size = weights_ref.shape[1]
    load = pltpu.make_async_copy(features_in_ref, features_ref, load_sems.at[0])
    load.start()
    ready = fetch_tiles(list_ref, weights_in_ref, weights_ref, sems)
    acc_ref[...] = jnp.zeros_like(acc_ref)
    weight_acc_ref[...] = jnp.zeros_like(weight_acc_ref)
    load.wait()

    def source_of(block):
        return features_ref[pl.ds(pl.multiple_of(block * size, size), size), :]

    stores = halves_out(acc_ref, acc_out_ref, load_sems)
    add_tiles(list_ref, weights_ref, source_of, acc_ref, weight_acc_ref, ready, stores[0].start)
    stores[1].start()
    row_sums(weight_acc_ref, sums_ref)
    for store in stores:
        store.wait()


def early_kernel(
    list_ref, border_ref, mine_ref, far_ref, other_ref, far_other_ref, weights_in_ref,
    acc_out_ref, sums_ref,
    weights_ref, acc_ref, weight_acc_ref, sources_ref, sems, load_sems,
):
    at, copies = 0, []
    for i, part in enumerate((border_ref, mine_ref, far_ref, other_ref, far_other_ref)):
        blocks = part.shape[0]
        copies.append(pltpu.make_async_copy(part, sources_ref.at[pl.ds(at, blocks)], load_sems.at[i]))
        at += blocks
    for copy in copies:
        copy.start()
    ready = fetch_tiles(list_ref, weights_in_ref, weights_ref, sems)
    acc_ref[...] = jnp.zeros_like(acc_ref)
    weight_acc_ref[...] = jnp.zeros_like(weight_acc_ref)
    for copy in copies:
        copy.wait()
    stores = halves_out(acc_ref, acc_out_ref, load_sems)
    add_tiles(list_ref, weights_ref, lambda i: sources_ref[i], acc_ref, weight_acc_ref, ready, stores[0].start)
    stores[1].start()
    row_sums(weight_acc_ref, sums_ref)
    for store in stores:
        store.wait()


def late_kernel(
    list_ref, place_ref, mine_ref, other_ref, own_in_ref, early_in_ref, weights_in_ref, features_in_ref,
    own_sums_ref, early_sums_ref, labels_ref, w_self_ref, w_neigh_ref, bias_in_ref, w_head_ref,
    keep_ref, send_ref,
    weights_ref, weight_acc_ref, acc_ref, own_ref, early_ref, features_ref, sources_ref, sums_ref, total_ref, bias_ref, head_ref,
    sems, load_sems, chunk_sems, *, scale,
):
    verts, width = features_ref.shape
    size = weights_ref.shape[1]
    blocks = mine_ref.shape[0]
    loads = [
        (mine_ref, sources_ref.at[pl.ds(0, blocks)]),
        (other_ref, sources_ref.at[pl.ds(blocks, blocks)]),
    ]
    copies = [pltpu.make_async_copy(a, b, load_sems.at[i]) for i, (a, b) in enumerate(loads)]
    for copy in copies:
        copy.start()
    ready = fetch_tiles(list_ref, weights_in_ref, weights_ref, sems)
    chunk_copies = []
    for i in range(verts // CHUNK):
        where = pl.ds(i * CHUNK, CHUNK)
        pairs = ((own_in_ref, own_ref), (early_in_ref, early_ref), (features_in_ref, features_ref))
        chunk_copies.append(
            [pltpu.make_async_copy(a.at[where], b.at[where], chunk_sems.at[i, j]) for j, (a, b) in enumerate(pairs)]
        )
        for copy in chunk_copies[-1]:
            copy.start()
    acc_ref[...] = jnp.zeros_like(acc_ref)
    weight_acc_ref[...] = jnp.zeros_like(weight_acc_ref)
    total_ref[...] = jnp.zeros_like(total_ref)
    bias_ref[...] = jnp.zeros_like(bias_ref)
    head_ref[...] = jnp.zeros_like(head_ref)
    w_self = split(w_self_ref[...])
    w_neigh = split(w_neigh_ref[...])
    w_head = w_head_ref[...]
    for copy in copies:
        copy.wait()
    add_tiles(list_ref, weights_ref, lambda i: sources_ref[i], acc_ref, weight_acc_ref, ready)
    row_sums(weight_acc_ref, sums_ref)
    inverse = 1.0 / (1.0 + (own_sums_ref[...] + early_sums_ref[...] + sums_ref[...]))
    target = 2.0 * labels_ref[...].astype(F32) - 1.0
    step = CHUNK // size

    def forward(i):
        where = pl.ds(i * CHUNK, CHUNK)
        own = features_ref[where, :]
        mean = (own + (acc_ref[where, :] + own_ref[where, :] + early_ref[where, :])) * as_columns(inverse[i * step : (i + 1) * step, :])
        own, mean = split(own), split(mean)
        pre = dot3(own, w_self) + dot3(mean, w_neigh) + bias_in_ref[...]
        sig = jax.nn.sigmoid(pre)
        hidden = pre * sig
        score = jnp.sum(hidden * w_head, axis=1, keepdims=True)
        dscore = (score - as_columns(target[i * step : (i + 1) * step, :])) * scale
        dpre = dscore * w_head * (sig * (1.0 + pre * (1.0 - sig)))
        bias_ref[...] += jnp.sum(dpre.reshape(CHUNK // 8, 8, width), axis=0)
        head_ref[...] += jnp.sum((hidden * dscore).reshape(CHUNK // 8, 8, width), axis=0)
        return own, mean, split(dpre)

    def backward(own, mean, dpre):
        total_ref[0:width, :] += dot3(own, dpre, ((0,), (0,)))
        total_ref[width : 2 * width, :] += dot3(mean, dpre, ((0,), (0,)))

    for first in range(0, verts // CHUNK, UNROLL):
        for i in range(first, first + UNROLL):
            for copy in chunk_copies[i]:
                copy.wait()
        for parts in [forward(i) for i in range(first, first + UNROLL)]:
            backward(*parts)

    me = place_ref[0]
    rows = 2 * width // 8
    extra = keep_ref.shape[1] - rows
    row_ids = lax.broadcasted_iota(jnp.int32, (extra, width), 0)
    vectors = jnp.where(row_ids == 0, jnp.sum(bias_ref[...], axis=0, keepdims=True), 0.0)
    vectors = jnp.where(row_ids == 1, jnp.sum(head_ref[...], axis=0, keepdims=True), vectors)
    for ref, away in ((keep_ref, 0), (send_ref, 4)):
        for j in range(4):
            piece = me ^ (away + j)
            ref[j, 0:rows, :] = total_ref[pl.ds(pl.multiple_of(piece * rows, rows), rows), :]
            ref[j, rows:, :] = jnp.where(piece == 0, vectors, 0.0)


def finish_kernel(place_ref, mine_ref, other_ref, self_ref, neigh_ref, bias_ref, head_ref):
    me = place_ref[0]
    width = self_ref.shape[1]
    rows = 2 * width // 8
    for ref, away in ((mine_ref, 0), (other_ref, 4)):
        for j in range(4):
            piece = me ^ (away + j)
            part = ref[j, 0:rows, :]
            at = pl.ds(pl.multiple_of(lax.rem(piece, 4) * rows, rows), rows)

            @pl.when(piece < 4)
            def _():
                self_ref[at, :] = part

            @pl.when(piece >= 4)
            def _():
                neigh_ref[at, :] = part

            @pl.when(piece == 0)
            def _():
                bias_ref[...] = ref[j, rows : rows + 1, :]
                head_ref[...] = ref[j, rows + 1 : rows + 2, :]


def keep_in(space, *arrays):
    return [pltpu.with_memory_space_constraint(array, space) for array in arrays]


def shape(*dims, dtype=F32):
    return jax.ShapeDtypeStruct(dims, dtype)


SMEM = pl.BlockSpec(memory_space=pltpu.SMEM)
VMEM = pl.BlockSpec(memory_space=pltpu.VMEM)
ANY = pl.BlockSpec(memory_space=pl.ANY)
HBM = pl.BlockSpec(memory_space=pltpu.HBM)


def on_device(
    peers,
    features,
    w_self,
    w_neigh,
    bias,
    w_head,
    tile_weights,
    tile_dst,
    tile_src,
    tile_count,
    hub_block,
    send_rows,
    send_count,
    labels,
):
    tiles, size, _ = tile_weights.shape
    verts, width = features.shape
    blocks = verts // size
    slots = send_rows.shape[2]
    border_blocks = peers * slots // size
    me = (lax.axis_index("vert") * lax.axis_size("row") + lax.axis_index("row")).astype(jnp.int32)

    bits = peers.bit_length() - 1
    core = 2
    line = [k << (bits - 2) for k in (1, 2, 3)]
    plane = [1 << b for b in range(bits - 2) if 1 << b != core]
    order = (plane[::-1], plane)

    def across(x, mask_of):
        return lax.ppermute(x, AXES, [(i, i ^ mask_of(i)) for i in range(peers)])

    source = tile_src.astype(jnp.int32)
    hub = jnp.clip(source - blocks - border_blocks, 0, peers - 1)
    apart = hub ^ me
    place_in_line = apart >> (bits - 2)
    sender_core = (hub >> 1) & 1
    steps = len(plane)

    def differs(s):
        return jnp.where(sender_core == 0, apart & order[0][s], apart & order[1][s]) != 0

    held_blocks, far_blocks = peers // 4, peers // 8
    index = place_in_line
    for s in range(steps - 1):
        index = index + jnp.where(differs(s), 4 << s, 0)
    through = differs(steps - 1)
    late = through & (index >= far_blocks)
    early_slot = border_blocks + index + jnp.where(through, held_blocks, 0)
    early_slot = early_slot + jnp.where((apart & core) != 0, held_blocks + far_blocks, 0)
    late_slot = index - far_blocks + jnp.where((apart & core) != 0, far_blocks, 0)
    stage = jnp.where(late, 2, 1)
    slot = jnp.where(late, late_slot, early_slot)
    at_border = source < blocks + border_blocks
    stage = jnp.where(source < blocks, 0, jnp.where(at_border, 1, stage))
    slot = jnp.where(source < blocks, source, jnp.where(at_border, source - blocks, slot))
    plan = (stage << 28) | (slot << 14) | (tile_dst << 8)
    alive = jnp.arange(slots, dtype=jnp.int32)[None, :] < send_count[0][:, None]
    listed = jnp.where(alive, send_rows[0], -1).reshape(-1)

    mine = lax.dynamic_slice_in_dim(features, hub_block[0] * size, size, 0)[None]
    held = jnp.concatenate([mine] + [across(mine, lambda i, m=m: m) for m in line], 0)

    features, tile_weights = keep_in(pltpu.HBM, features, tile_weights)
    index_list = shape(tiles + 8, dtype=jnp.int32)
    outgoing, own_list, early_list, late_list = pl.pallas_call(
        functools.partial(prepare_kernel, size=size),
        out_shape=(shape(peers, slots, width),) + (index_list,) * 3,
        in_specs=[SMEM] * 3 + [HBM],
        out_specs=(VMEM, SMEM, SMEM, SMEM),
        scratch_shapes=[pltpu.VMEM((verts, width), F32), pltpu.SemaphoreType.DMA((1,))],
        compiler_params=pltpu.CompilerParams(vmem_limit_bytes=VMEM_BYTES),
        cost_estimate=COST,
        name="prepare",
    )(*keep_in(pltpu.HBM, plan, listed), tile_count, features)
    held, outgoing, own_list = lax.optimization_barrier((held, outgoing, own_list))

    own_acc, own_sums = pl.pallas_call(
        own_kernel,
        out_shape=(pltpu.HBM((verts, width), F32), shape(blocks, size)),
        in_specs=[SMEM, HBM, HBM],
        out_specs=(HBM, VMEM),
        scratch_shapes=[
            pltpu.VMEM((verts, width), F32),
            pltpu.VMEM((tiles, size, size), F32),
            pltpu.VMEM((verts, width), F32),
            pltpu.VMEM((blocks, size, size), F32),
            pltpu.SemaphoreType.DMA((tiles // GROUP,)),
            pltpu.SemaphoreType.DMA((2,)),
        ],
        compiler_params=pltpu.CompilerParams(vmem_limit_bytes=VMEM_BYTES),
        cost_estimate=COST,
        name="own_tiles",
    )(own_list, features, tile_weights)

    incoming = lax.all_to_all(outgoing, AXES, split_axis=0, concat_axis=0, tiled=True)
    border = incoming.reshape(border_blocks, size, width)

    for s in range(steps - 1):
        near = held
        held = jnp.concatenate([held, across(held, lambda i, s=s: order[(i >> 1) & 1][s])], 0)
    far_near = across(near, lambda i: order[(i >> 1) & 1][steps - 1])
    held, far_near, border, own_sums = lax.optimization_barrier((held, far_near, border, own_sums))
    far = across(held[far_blocks:], lambda i: order[(i >> 1) & 1][steps - 1])
    held_other = across(held, lambda i: core)
    far_near_other = across(far_near, lambda i: core)

    early_acc, early_sums = pl.pallas_call(
        early_kernel,
        out_shape=(pltpu.HBM((verts, width), F32), shape(blocks, size)),
        in_specs=[SMEM] + [ANY] * 5 + [HBM],
        out_specs=(HBM, VMEM),
        scratch_shapes=[
            pltpu.VMEM((tiles, size, size), F32),
            pltpu.VMEM((verts, width), F32),
            pltpu.VMEM((blocks, size, size), F32),
            pltpu.VMEM((border_blocks + 2 * (held_blocks + far_blocks), size, width), F32),
            pltpu.SemaphoreType.DMA((tiles // GROUP,)),
            pltpu.SemaphoreType.DMA((5,)),
        ],
        compiler_params=pltpu.CompilerParams(vmem_limit_bytes=VMEM_BYTES),
        cost_estimate=COST,
        name="early_tiles",
    )(early_list, border, held, far_near, held_other, far_near_other, tile_weights)
    far, early_sums = lax.optimization_barrier((far, early_sums))
    far_other = across(far, lambda i: core)

    place = ((me >> 1) & 1) * 4 + ((me >> 2) & 1) * 2 + (me & 1)
    place = place.reshape(1)
    piece_rows = 2 * width // 8 + 8
    keep, send = pl.pallas_call(
        functools.partial(late_kernel, scale=1.0 / math.sqrt(verts * peers)),
        out_shape=(shape(4, piece_rows, width), shape(4, piece_rows, width)),
        in_specs=[SMEM, SMEM, ANY, ANY] + [HBM] * 4 + [VMEM] * 7,
        out_specs=(VMEM, VMEM),
        scratch_shapes=[
            pltpu.VMEM((tiles, size, size), F32),
            pltpu.VMEM((blocks, size, size), F32),
            pltpu.VMEM((verts, width), F32),
            pltpu.VMEM((verts, width), F32),
            pltpu.VMEM((verts, width), F32),
            pltpu.VMEM((verts, width), F32),
            pltpu.VMEM((2 * far_blocks, size, width), F32),
            pltpu.VMEM((blocks, size), F32),
            pltpu.VMEM((2 * width, width), F32),
            pltpu.VMEM((8, width), F32),
            pltpu.VMEM((8, width), F32),
            pltpu.SemaphoreType.DMA((tiles // GROUP,)),
            pltpu.SemaphoreType.DMA((2,)),
            pltpu.SemaphoreType.DMA((verts // CHUNK, 3)),
        ],
        compiler_params=pltpu.CompilerParams(vmem_limit_bytes=VMEM_BYTES),
        cost_estimate=COST,
        name="late_tiles_and_gradients",
    )(
        late_list, place, far, far_other,
        *keep_in(pltpu.HBM, own_acc, early_acc), tile_weights, features,
        own_sums, early_sums, labels.reshape(blocks, size),
        w_self, w_neigh, bias.reshape(1, width), w_head.reshape(1, width),
    )

    held = keep + across(send, lambda i: core)
    reach = (0, 1, 4, 5)
    got = [held[0]] + [across(held[j], lambda i, j=j: reach[j]) for j in (1, 2, 3)]
    total = (got[0] + got[1]) + (got[2] + got[3])
    for low in range(3, bits, 2):
        masks = [1 << low] if low + 1 == bits else [k << low for k in (1, 2, 3)]
        more = [across(total, lambda i, m=m: m) for m in masks]
        total = total + more[0] if len(more) == 1 else (total + more[0]) + (more[1] + more[2])
    mine = jnp.stack([total] + [across(total, lambda i, j=j: reach[j]) for j in (1, 2, 3)])
    other = across(mine, lambda i: core)
    grad_self, grad_neigh, grad_bias, grad_head = pl.pallas_call(
        finish_kernel,
        out_shape=(shape(width, width), shape(width, width), shape(1, width), shape(1, width)),
        in_specs=[SMEM, VMEM, VMEM],
        out_specs=(VMEM, VMEM, VMEM, VMEM),
        name="assemble",
    )(place, *keep_in(pltpu.VMEM, mine, other))
    return (grad_self, grad_neigh, grad_bias.reshape(width), grad_head.reshape(width))


def solution(mesh):
    peers = math.prod(mesh.shape.values())
    in_specs = (
        P(AXES, None),
        P(),
        P(),
        P(),
        P(),
        P(AXES, None, None),
        P(AXES),
        P(AXES),
        P(AXES),
        P(AXES),
        P(AXES, None, None),
        P(AXES, None),
        P(AXES),
    )
    out_specs = (P(), P(), P(), P())
    return jax.shard_map(
        functools.partial(on_device, peers),
        mesh=mesh,
        in_specs=in_specs,
        out_specs=out_specs,
        check_vma=False,
    )
```
